32 devices in a mesh: inp: 4 (over z), out: 4 (over y, core), dep: 2 (over x).
Axes of the slice: x: 2, y: 2, z: 4, core: 2. Of those that a mesh axis runs over, the one named last changes fastest.
Arguments:
- tokens: bfloat16 [384, 8192], P('dep', 'inp'), may hold values from -6 to 6
- grad_hidden: bfloat16 [384, 14336], P('dep', 'out'), may hold values from -3 to 3
- w_gate: bfloat16 [8192, 14336], P('inp', 'out'), may hold values from -0.0625 to 0.0625
- w_up: bfloat16 [8192, 14336], P('inp', 'out'), may hold values from -0.0625 to 0.0625
Outputs:
- grad_input: bfloat16 [384, 8192], P('dep', ('inp', 'out'))
- gate_grad: bfloat16 [8192, 14336], P(('inp', 'dep'), 'out')
- up_grad: bfloat16 [8192, 14336], P(('inp', 'dep'), 'out')
The draws below stay inside these ranges and needn't reach their ends.
All inputs are finite; a program needn't handle non-finite values.
Results may differ from the reference program's by a relative error of at most 0.019.
Values may be sent and summed in bfloat16 or wider, within the bound.
A program may use at most 128 MiB of HBM per device.

```python
import math
import jax
import jax.numpy as jnp
from jax import lax

D = 8192
FF = 14336
TOK_DEP = 192
TOKENS = 384
N_DEP = 2


def with_spikes(array, stream_key, source, target, parts, factor):
    def block_of(axis_at):
        return (jnp.arange(array.shape[axis_at]) // (array.shape[axis_at] // parts)).reshape((-1,) + (1,) * (array.ndim - 1 - axis_at))

    first = jax.random.permutation(stream_key, parts)[block_of(target)]
    far = (block_of(target) + parts // 2) % parts
    return jnp.where((block_of(source) == first) | (block_of(source) == far), factor * array, array)


def block_scale(key, shape, split, low, top_value):
    def one(axis_at, blocks):
        steps = jax.random.uniform(jax.random.fold_in(jax.random.fold_in(key, 6), axis_at), (blocks,), jnp.float32, low / len(split), top_value / len(split))
        return jnp.repeat(jnp.exp(steps), shape[axis_at] // blocks).reshape((-1,) + (1,) * (len(shape) - axis_at - 1))

    level = one(*split[0])
    for cut in split[1:]:
        level = level * one(*cut)
    return level


def gaussian(own_key, dims, scale, bound, cuts=(), dtype=jnp.bfloat16):
    gain = block_scale(own_key, dims, cuts, -0.22, 0.18) if cuts else 1.0
    values = jax.random.normal(own_key, dims, jnp.float32) * scale * gain
    return jnp.minimum(jnp.maximum(values, -bound), bound).astype(dtype)


def bell_draw_with(rng, extent, spread, limit, split, heavy, dtype=jnp.bfloat16):
    values = spread * jax.random.normal(rng, extent, jnp.float32)
    if split:
        values = values * block_scale(rng, extent, split, -0.22, 0.18)
    return jnp.clip(with_spikes(values, jax.random.fold_in(rng, 3), *heavy), -limit, limit).astype(dtype)


def setup_inputs(seed: int = 0) -> dict:
    seeds = jax.random.split(jax.random.key(seed), 5)
    tokens = bell_draw_with(seeds[0], (TOKENS, D), 1.0, 6.0, ((0, 2), (1, 4)), (0, 1, 4, 2.0))
    grad_hidden = gaussian(seeds[1], (TOKENS, FF), 0.5, 3.0, ((0, 2), (1, 4)))
    w_gate = gaussian(seeds[2], (D, FF), D ** -0.5, 0.0625, ((0, 4), (1, 4)))
    w_up = gaussian(seeds[3], (D, FF), D ** -0.5, 0.0625, ((0, 4), (1, 4)))
    return {"tokens": tokens, "grad_hidden": grad_hidden, "w_gate": w_gate, "w_up": w_up}


def contract_rows(left, right):
    return lax.dot_general(left, right, (((0,), (0,)), ((), ())), preferred_element_type=jnp.float32)

def contract_cols(left, right):
    return lax.dot_general(left, right, (((1,), (1,)), ((), ())), preferred_element_type=jnp.float32)

def reference(tokens, grad_hidden, w_gate, w_up):
    gate_value = jnp.dot(tokens, w_gate, preferred_element_type=jnp.float32)
    up_value = jnp.dot(tokens, w_up, preferred_element_type=jnp.float32)
    sigmoid_gate = jax.nn.sigmoid(gate_value)
    cotangent = grad_hidden.astype(jnp.float32)
    grad_gate = (cotangent * up_value * sigmoid_gate * (1.0 + gate_value * (1.0 - sigmoid_gate))).astype(jnp.bfloat16)
    grad_up = (cotangent * gate_value * sigmoid_gate).astype(jnp.bfloat16)
    grad_input = (contract_cols(grad_gate, w_gate) + contract_cols(grad_up, w_up)).astype(jnp.bfloat16)
    gate_total = jnp.zeros((D, FF), jnp.float32)
    up_total = jnp.zeros((D, FF), jnp.float32)
    for block_index in range(N_DEP):
        first_row = block_index * TOK_DEP
        token_block = tokens[first_row:first_row + TOK_DEP]
        gate_part = contract_rows(token_block, grad_gate[first_row:first_row + TOK_DEP]).astype(jnp.bfloat16)
        up_part = contract_rows(token_block, grad_up[first_row:first_row + TOK_DEP]).astype(jnp.bfloat16)
        gate_part = lax.optimization_barrier(gate_part)
        up_part = lax.optimization_barrier(up_part)
        gate_total = gate_total + gate_part.astype(jnp.float32)
        up_total = up_total + up_part.astype(jnp.float32)
    factor = 1.0 / math.sqrt(TOKENS)
    return (grad_input, (gate_total * factor).astype(jnp.bfloat16), (up_total * factor).astype(jnp.bfloat16))
```

```python
import math

import jax
import jax.numpy as jnp
from jax import lax
from jax.sharding import PartitionSpec as P


def local_product(left, right):
    return jnp.dot(left, right, preferred_element_type=jnp.float32)


def contract_rows(left, right):
    return lax.dot_general(
        left, right, (((0,), (0,)), ((), ())), preferred_element_type=jnp.float32
    )


def contract_cols(left, right):
    return lax.dot_general(
        left, right, (((1,), (1,)), ((), ())), preferred_element_type=jnp.float32
    )


def shards(tokens, grad_hidden, w_gate, w_up):
    token_count = tokens.shape[0]
    own_rows = token_count // lax.axis_size("inp")
    hidden_width = w_gate.shape[1]
    factor = 1.0 / math.sqrt(token_count * lax.axis_size("dep"))
    summed = lax.psum_scatter(
        jnp.concatenate(
            [local_product(tokens, w_gate), local_product(tokens, w_up)], axis=1
        ).astype(jnp.bfloat16),
        "inp",
        scatter_dimension=0,
        tiled=True,
    )
    summed = summed.astype(jnp.float32)
    gate_value = summed[:, :hidden_width]
    up_value = summed[:, hidden_width:]
    offset = lax.axis_index("inp") * own_rows
    cotangent = lax.dynamic_slice_in_dim(grad_hidden, offset, own_rows, 0).astype(jnp.float32)
    sigmoid_gate = jax.nn.sigmoid(gate_value)
    grad_gate = (
        cotangent * up_value * sigmoid_gate * (1.0 + gate_value * (1.0 - sigmoid_gate))
    ).astype(jnp.bfloat16)
    grad_upper = (cotangent * gate_value * sigmoid_gate).astype(jnp.bfloat16)
    paired = jnp.concatenate([grad_gate, grad_upper], axis=1)
    gathered = lax.all_gather(paired, "inp", axis=0, tiled=True)
    full_gate = gathered[:, :hidden_width]
    full_upper = gathered[:, hidden_width:]
    input_terms = contract_cols(full_gate, w_gate) + contract_cols(full_upper, w_up)
    grad_input = lax.psum_scatter(input_terms, "out", scatter_dimension=1, tiled=True).astype(
        jnp.bfloat16
    )
    dep_count = lax.axis_size("dep")
    every_token = lax.all_gather(tokens, "dep", axis=0, tiled=True)
    own_features = tokens.shape[1] // dep_count
    own_tokens = lax.dynamic_slice_in_dim(
        every_token, lax.axis_index("dep") * own_features, own_features, 1
    )
    every_grad = lax.all_gather(gathered, "dep", axis=0, tiled=True)
    weight_grad = (contract_rows(own_tokens, every_grad) * factor).astype(jnp.bfloat16)
    return grad_input, weight_grad[:, :hidden_width], weight_grad[:, hidden_width:]


def solution(mesh):
    return jax.shard_map(
        shards,
        mesh=mesh,
        in_specs=(P("dep", "inp"), P("dep", "out"), P("inp", "out"), P("inp", "out")),
        out_specs=(P("dep", ("inp", "out")), P(("inp", "dep"), "out"), P(("inp", "dep"), "out")),
        check_vma=False,
    )
```

```python
import math

import jax
import jax.numpy as jnp
from jax import lax
from jax.sharding import PartitionSpec as P

CHUNKS = 2


def local_product(left, right):
    return jnp.dot(left, right, preferred_element_type=jnp.float32)


def contract_rows(left, right):
    return lax.dot_general(
        left, right, (((0,), (0,)), ((), ())), preferred_element_type=jnp.float32
    )


def contract_cols(left, right):
    return lax.dot_general(
        left, right, (((1,), (1,)), ((), ())), preferred_element_type=jnp.float32
    )


def activation_grads(gate_value, up_value, cotangent):
    sigmoid_gate = jax.nn.sigmoid(gate_value)
    grad_gate = cotangent * up_value * sigmoid_gate * (1.0 + gate_value * (1.0 - sigmoid_gate))
    grad_upper = cotangent * gate_value * sigmoid_gate
    return jnp.concatenate(
        [grad_gate.astype(jnp.bfloat16), grad_upper.astype(jnp.bfloat16)], axis=1
    )


def shards(tokens, grad_hidden, w_gate, w_up):
    token_count = tokens.shape[0]
    own_rows = token_count // lax.axis_size("inp")
    chunk = w_gate.shape[1] // CHUNKS
    dep_count = lax.axis_size("dep")
    dep_index = lax.axis_index("dep")
    factor = 1.0 / math.sqrt(token_count * dep_count)
    offset = lax.axis_index("inp") * own_rows
    cotangent = lax.dynamic_slice_in_dim(grad_hidden, offset, own_rows, 0).astype(jnp.float32)

    own_features = tokens.shape[1] // dep_count
    every_token = lax.all_gather(tokens, "dep", axis=0, tiled=True)
    own_tokens = lax.dynamic_slice_in_dim(every_token, dep_index * own_features, own_features, 1)

    every_grad = []
    for step in range(CHUNKS):
        columns = slice(step * chunk, (step + 1) * chunk)
        partial = jnp.concatenate(
            [local_product(tokens, w_gate[:, columns]), local_product(tokens, w_up[:, columns])],
            axis=1,
        ).astype(jnp.bfloat16)
        summed = lax.psum_scatter(partial, "inp", scatter_dimension=0, tiled=True)
        summed = summed.astype(jnp.float32)
        paired = activation_grads(summed[:, :chunk], summed[:, chunk:], cotangent[:, columns])
        every_grad.append(lax.all_gather(paired, ("dep", "inp"), axis=0, tiled=True))

    input_terms = 0.0
    for step, both in enumerate(every_grad):
        columns = slice(step * chunk, (step + 1) * chunk)
        own = lax.dynamic_slice_in_dim(both, dep_index * token_count, token_count, 0)
        input_terms += contract_cols(own[:, :chunk], w_gate[:, columns])
        input_terms += contract_cols(own[:, chunk:], w_up[:, columns])
    grad_input = lax.psum_scatter(
        input_terms.astype(jnp.bfloat16), "out", scatter_dimension=1, tiled=True
    )
    every_gate = jnp.concatenate([both[:, :chunk] for both in every_grad], axis=1)
    every_upper = jnp.concatenate([both[:, chunk:] for both in every_grad], axis=1)
    return (
        grad_input,
        (contract_rows(own_tokens, every_gate) * factor).astype(jnp.bfloat16),
        (contract_rows(own_tokens, every_upper) * factor).astype(jnp.bfloat16),
    )


def solution(mesh):
    return jax.shard_map(
        shards,
        mesh=mesh,
        in_specs=(P("dep", "inp"), P("dep", "out"), P("inp", "out"), P("inp", "out")),
        out_specs=(P("dep", ("inp", "out")), P(("inp", "dep"), "out"), P(("inp", "dep"), "out")),
        check_vma=False,
    )
```

```python
import math

import jax
import jax.numpy as jnp
from jax import lax
from jax.sharding import PartitionSpec as P

CHUNKS = 2


def local_product(left, right):
    return jnp.dot(left, right, preferred_element_type=jnp.float32)


def contract_rows(left, right):
    return lax.dot_general(
        left, right, (((0,), (0,)), ((), ())), preferred_element_type=jnp.float32
    )


def contract_cols(left, right):
    return lax.dot_general(
        left, right, (((1,), (1,)), ((), ())), preferred_element_type=jnp.float32
    )


def activation_grads(gate_value, up_value, cotangent):
    sigmoid_gate = jax.nn.sigmoid(gate_value)
    grad_gate = cotangent * up_value * sigmoid_gate * (1.0 + gate_value * (1.0 - sigmoid_gate))
    grad_upper = cotangent * gate_value * sigmoid_gate
    return jnp.concatenate(
        [grad_gate.astype(jnp.bfloat16), grad_upper.astype(jnp.bfloat16)], axis=1
    )


def shards(tokens, grad_hidden, w_gate, w_up):
    token_count = tokens.shape[0]
    own_rows = token_count // lax.axis_size("inp")
    chunk = w_gate.shape[1] // CHUNKS
    dep_count = lax.axis_size("dep")
    dep_index = lax.axis_index("dep")
    factor = 1.0 / math.sqrt(token_count * dep_count)
    offset = lax.axis_index("inp") * own_rows
    cotangent = lax.dynamic_slice_in_dim(grad_hidden, offset, own_rows, 0).astype(jnp.float32)

    own_features = tokens.shape[1] // dep_count

    def token_columns(owner):
        return lax.dynamic_slice_in_dim(tokens, owner * own_features, own_features, 1)

    def shifted(array, shift):
        return lax.ppermute(array, "dep", [(i, (i + shift) % dep_count) for i in range(dep_count)])

    shifts = range(1, dep_count)
    every_token = jnp.concatenate(
        [token_columns(dep_index)]
        + [shifted(token_columns((dep_index + shift) % dep_count), shift) for shift in shifts],
        axis=0,
    )

    every_grad = []
    for step in range(CHUNKS):
        columns = slice(step * chunk, (step + 1) * chunk)
        partial = jnp.concatenate(
            [local_product(tokens, w_gate[:, columns]), local_product(tokens, w_up[:, columns])],
            axis=1,
        ).astype(jnp.bfloat16)
        summed = lax.psum_scatter(partial, "inp", scatter_dimension=0, tiled=True)
        summed = summed.astype(jnp.float32)
        paired = activation_grads(summed[:, :chunk], summed[:, chunk:], cotangent[:, columns])
        every_grad.append(lax.all_gather(paired, "inp", axis=0, tiled=True))

    input_terms = 0.0
    for step, own in enumerate(every_grad):
        columns = slice(step * chunk, (step + 1) * chunk)
        input_terms += contract_cols(own[:, :chunk], w_gate[:, columns])
        input_terms += contract_cols(own[:, chunk:], w_up[:, columns])
    grad_input = lax.psum_scatter(
        input_terms.astype(jnp.bfloat16), "out", scatter_dimension=1, tiled=True
    )
    by_owner = [every_grad] + [[shifted(own, shift) for own in every_grad] for shift in shifts]
    every_gate = jnp.concatenate(
        [jnp.concatenate([both[:, :chunk] for both in chunks], axis=1) for chunks in by_owner], axis=0
    )
    every_upper = jnp.concatenate(
        [jnp.concatenate([both[:, chunk:] for both in chunks], axis=1) for chunks in by_owner], axis=0
    )
    return (
        grad_input,
        (contract_rows(every_token, every_gate) * factor).astype(jnp.bfloat16),
        (contract_rows(every_token, every_upper) * factor).astype(jnp.bfloat16),
    )


def solution(mesh):
    return jax.shard_map(
        shards,
        mesh=mesh,
        in_specs=(P("dep", "inp"), P("dep", "out"), P("inp", "out"), P("inp", "out")),
        out_specs=(P("dep", ("inp", "out")), P(("inp", "dep"), "out"), P(("inp", "dep"), "out")),
        check_vma=False,
    )
```
